512 devices in a mesh: patch: 128 (over y, z, core), lat: 4 (over x).
Axes of the slice: x: 4, y: 8, z: 8, core: 2. Of those that a mesh axis runs over, the one named last changes fastest.
Arguments:
- nodes: bfloat16 [32768, 512], P('patch', 'lat'), may hold values from -6 to 6
- short_edges: bfloat16 [131072, 512], P(('patch', 'lat')), may hold values from -6 to 6
- long_edges: bfloat16 [65536, 512], P(('patch', 'lat')), may hold values from -6 to 6
- short_send: int32 [131072], P(('patch', 'lat')), may hold values from 0 to 511
- short_recv: int32 [131072], P(('patch', 'lat')), may hold values from 0 to 63
- long_send: int32 [65536], P(('patch', 'lat')), may hold values from 0 to 255
- long_recv: int32 [65536], P(('patch', 'lat')), may hold values from 0 to 63
- send_rows: int32 [128, 128, 2], P('patch'), may hold values from 0 to 15
- tile_rows: int32 [128, 128, 2], P('patch'), may hold values from 0 to 255
- edge_w_in: bfloat16 [1536, 512], replicated, may hold values from -0.15625 to 0.15625
- edge_b_in: float32 [512], replicated, may hold values from -3 to 3
- edge_w_out: bfloat16 [512, 512], replicated, may hold values from -0.25 to 0.25
- edge_b_out: float32 [512], replicated, may hold values from -3 to 3
- edge_gain: float32 [512], replicated, may hold values from 0.5 to 1.5
- edge_shift: float32 [512], replicated, may hold values from -3 to 3
- node_w_in: bfloat16 [1024, 512], replicated, may hold values from -0.1875 to 0.1875
- node_b_in: float32 [512], replicated, may hold values from -3 to 3
- node_w_out: bfloat16 [512, 512], replicated, may hold values from -0.25 to 0.25
- node_b_out: float32 [512], replicated, may hold values from -3 to 3
- node_gain: float32 [512], replicated, may hold values from 0.5 to 1.5
- node_shift: float32 [512], replicated, may hold values from -3 to 3
Outputs:
- short_new: bfloat16 [131072, 512], P(('patch', 'lat'))
- long_new: bfloat16 [65536, 512], P(('patch', 'lat'))
- new_nodes: bfloat16 [32768, 512], P('patch', 'lat')
- tiles: bfloat16 [32768, 512], P('patch', 'lat')
The draws below stay inside these ranges and needn't reach their ends.
Inputs may be any that keep to these rules, and one draw needn't show every extreme that they name: `send_rows`: coarse rows are the first 16 rows of a patch.
All inputs are finite; a program needn't handle non-finite values.
Results may differ from the reference program's by a relative error of at most 0.005.
Values may be sent and summed in bfloat16 or wider, within the bound.
No kernel may reach another device: no remote copies, remote signals or barrier semaphores. Data moves between devices by JAX's collectives and lax.ppermute only.
A program may use at most 64 MiB of HBM per device.

```python
import jax
import jax.numpy as jnp
from jax import lax

D = 512
NODE_DEV = 256
ES_DEV = 256
EL_DEV = 128
COARSE_DEV = 16
LCAP = 2
TILE_DEV = 256
HALO = 128
QUARTER = 64
NODES = 32768
SHORT = 131072
LONG = 65536
DCAP = 2
N_PATCH = 128
N_LAT = 4


def set_ends(result, key, smallest, largest):
    extent = result.shape
    place = [jax.random.randint(jax.random.fold_in(key, axis), (), 0, extent[axis]) for axis in range(len(extent))]
    result = result.at[tuple(place)].set(smallest)
    longest = extent.index(max(extent))
    place[longest] = (place[longest] + 1) % extent[longest]
    return result.at[tuple(place)].set(largest)


def steps_of(key, extent, cuts, least, high):
    loudness, own = 1.0, jax.random.fold_in(key, 6)
    for axis_at, shards_of in cuts:
        draws = jnp.exp(jax.random.uniform(jax.random.fold_in(own, axis_at), (shards_of,), jnp.float32, least / len(cuts), high / len(cuts)))
        loudness = loudness * jnp.repeat(draws, extent[axis_at] // shards_of).reshape([-1 if axis == axis_at else 1 for axis in range(len(extent))])
    return loudness


def normal_values(rng, dims, scale, limit, shards=(), kind=jnp.bfloat16):
    array = scale * jax.random.normal(rng, dims, jnp.float32)
    if shards:
        array = array * steps_of(rng, dims, shards, -0.22, 0.18)
    return jnp.clip(array, -limit, limit).astype(kind)


def setup_inputs(seed: int = 0) -> dict:
    key_list = jax.random.split(jax.random.key(seed), 22)
    return {
        "nodes": normal_values(key_list[0], (NODES, D), 1.0, 6.0, ((0, 128), (1, 4))),
        "short_edges": normal_values(key_list[1], (SHORT, D), 1.0, 6.0, ((0, 512),)),
        "long_edges": normal_values(key_list[2], (LONG, D), 1.0, 6.0, ((0, 512),)),
        "short_send": set_ends(jax.random.randint(key_list[3], (SHORT,), 0, NODE_DEV + 2 * HALO), jax.random.fold_in(key_list[3], 1), 0, (NODE_DEV + 2 * HALO) - 1).astype(jnp.int32),
        "short_recv": set_ends(jax.random.randint(key_list[4], (SHORT,), 0, QUARTER), jax.random.fold_in(key_list[4], 1), 0, QUARTER - 1).astype(jnp.int32),
        "long_send": set_ends(jax.random.randint(key_list[5], (LONG,), 0, N_PATCH * LCAP), jax.random.fold_in(key_list[5], 1), 0, (N_PATCH * LCAP) - 1).astype(jnp.int32),
        "long_recv": set_ends(jax.random.randint(key_list[6], (LONG,), 0, QUARTER), jax.random.fold_in(key_list[6], 1), 0, QUARTER - 1).astype(jnp.int32),
        "send_rows": set_ends(jax.random.randint(key_list[7], (N_PATCH, N_PATCH, LCAP), 0, COARSE_DEV), jax.random.fold_in(key_list[7], 1), 0, COARSE_DEV - 1).astype(jnp.int32),
        "tile_rows": set_ends(jax.random.randint(key_list[8], (N_PATCH, N_PATCH, DCAP), 0, NODE_DEV), jax.random.fold_in(key_list[8], 1), 0, NODE_DEV - 1).astype(jnp.int32),
        "edge_w_in": normal_values(key_list[9], (3 * D, D), (3 * D) ** -0.5, 0.15625),
        "edge_b_in": normal_values(key_list[10], (D,), 0.5, 3.0, (), jnp.float32),
        "edge_w_out": normal_values(key_list[11], (D, D), D ** -0.5, 0.25),
        "edge_b_out": normal_values(key_list[12], (D,), 0.5, 3.0, (), jnp.float32),
        "edge_gain": jnp.clip(1.0 + 0.1 * jax.random.normal(key_list[13], (D,), jnp.float32), 0.5, 1.5),
        "edge_shift": normal_values(key_list[14], (D,), 0.5, 3.0, (), jnp.float32),
        "node_w_in": normal_values(key_list[15], (2 * D, D), (2 * D) ** -0.5, 0.1875),
        "node_b_in": normal_values(key_list[16], (D,), 0.5, 3.0, (), jnp.float32),
        "node_w_out": normal_values(key_list[17], (D, D), D ** -0.5, 0.25),
        "node_b_out": normal_values(key_list[18], (D,), 0.5, 3.0, (), jnp.float32),
        "node_gain": jnp.clip(1.0 + 0.1 * jax.random.normal(key_list[19], (D,), jnp.float32), 0.5, 1.5),
        "node_shift": normal_values(key_list[20], (D,), 0.5, 3.0, (), jnp.float32),
    }


def norm_rows(values, gain_row, shift_row):
    average = lax.optimization_barrier(jnp.mean(values, axis=-1, keepdims=True))
    centered = values - average
    variance = lax.optimization_barrier(jnp.mean(centered * centered, axis=-1, keepdims=True))
    return centered * lax.rsqrt(variance + 1e-05) * gain_row + shift_row

def reference(nodes, short_edges, long_edges, short_send, short_recv, long_send, long_recv, send_rows, tile_rows, edge_w_in, edge_b_in, edge_w_out, edge_b_out, edge_gain, edge_shift, node_w_in, node_b_in, node_w_out, node_b_out, node_gain, node_shift):
    quarter = NODE_DEV // N_LAT
    short_block = jnp.arange(SHORT, dtype=jnp.int32) // ES_DEV
    short_patch = short_block // N_LAT
    short_lat = short_block % N_LAT
    short_src = (short_patch * NODE_DEV + short_send - HALO) % NODES
    short_dst = short_patch * NODE_DEV + short_lat * quarter + short_recv
    long_block = jnp.arange(LONG, dtype=jnp.int32) // EL_DEV
    long_patch = long_block // N_LAT
    long_lat = long_block % N_LAT
    source = long_send // LCAP
    slot_index = long_send % LCAP
    long_src = source * NODE_DEV + send_rows[source, long_patch, slot_index]
    long_dst = long_patch * NODE_DEV + long_lat * quarter + long_recv
    w_self = edge_w_in[:D]
    send_proj = jnp.dot(nodes, edge_w_in[D:2 * D], preferred_element_type=jnp.float32)
    recv_proj = jnp.dot(nodes, edge_w_in[2 * D:], preferred_element_type=jnp.float32)

    def update(edges, senders, receivers):
        before = jnp.dot(edges, w_self, preferred_element_type=jnp.float32) + send_proj[senders] + recv_proj[receivers] + edge_b_in
        hidden = jax.nn.silu(before).astype(jnp.bfloat16)
        output = jnp.dot(hidden, edge_w_out, preferred_element_type=jnp.float32) + edge_b_out
        return (edges.astype(jnp.float32) + norm_rows(output, edge_gain, edge_shift)).astype(jnp.bfloat16)
    short_new = update(short_edges, short_src, short_dst)
    long_new = update(long_edges, long_src, long_dst)
    aggregate = jax.ops.segment_sum(short_new.astype(jnp.float32), short_dst, NODES)
    aggregate = aggregate + jax.ops.segment_sum(long_new.astype(jnp.float32), long_dst, NODES)
    aggregate = aggregate.astype(jnp.bfloat16)
    before = jnp.dot(nodes, node_w_in[:D], preferred_element_type=jnp.float32)
    before = before + jnp.dot(aggregate, node_w_in[D:], preferred_element_type=jnp.float32) + node_b_in
    hidden = jax.nn.silu(before).astype(jnp.bfloat16)
    output = jnp.dot(hidden, node_w_out, preferred_element_type=jnp.float32) + node_b_out
    new_nodes = (nodes.astype(jnp.float32) + norm_rows(output, node_gain, node_shift)).astype(jnp.bfloat16)
    tile_pos = jnp.arange(TILE_DEV, dtype=jnp.int32)
    tile_src = tile_pos // DCAP
    tile_slot = tile_pos % DCAP
    owners = jnp.arange(N_PATCH, dtype=jnp.int32)[:, None]
    tile_index = tile_src[None, :] * NODE_DEV + tile_rows[tile_src[None, :], owners, tile_slot[None, :]]
    tiles = new_nodes[tile_index.reshape(-1)]
    return (short_new, long_new, new_nodes, tiles)
```

```python
import functools

import jax
import jax.numpy as jnp
from jax import lax
from jax.experimental import pallas as pl
from jax.experimental.pallas import tpu as pltpu
from jax.sharding import PartitionSpec as P

HALO = 128
LANES = 128
F32 = jnp.float32
BF16 = jnp.bfloat16


def matmul(a, b):
    return jnp.dot(a, b, preferred_element_type=F32)


def silu(v):
    return v / (1.0 + jnp.exp(-v))


def norm_rows(values, gain_row, shift_row):
    average = jnp.mean(values, axis=-1, keepdims=True)
    centered = values - average
    variance = jnp.mean(centered * centered, axis=-1, keepdims=True)
    return centered * lax.rsqrt(variance + 1e-05) * gain_row + shift_row


def column(row):
    shape = (LANES, LANES)
    same = lax.broadcasted_iota(jnp.int32, shape, 0) == lax.broadcasted_iota(jnp.int32, shape, 1)
    return jnp.sum(jnp.where(same, row.astype(F32), 0.0), axis=1, keepdims=True)


def columns(rows):
    return jnp.concatenate([column(rows[i : i + 1]) for i in range(rows.shape[0])], axis=0)


def pick(index_column, count):
    shape = (index_column.shape[0], count)
    places = lax.broadcasted_iota(jnp.int32, shape, 1).astype(F32)
    return jnp.where(places == index_column, 1.0, 0.0).astype(BF16)


def spread(index_rows, repeat):
    shape = (LANES * repeat, LANES)
    line = lax.broadcasted_iota(jnp.int32, shape, 0)
    patch = lax.broadcasted_iota(jnp.int32, shape, 1)
    here = lax.div(line, repeat) == patch
    odd = lax.rem(line, 2) == 1
    values = jnp.where(odd, index_rows[1:2].astype(F32), index_rows[0:1].astype(F32))
    return jnp.sum(jnp.where(here, values, 0.0), axis=1, keepdims=True)


def far_kernel(full_ref, rows_ref, out_ref, coarse, *, coarse_rows):
    chunks = full_ref.shape[0]
    per = 2 * chunks
    for c in range(chunks):
        coarse[c * coarse_rows : (c + 1) * coarse_rows, :] = full_ref[c, :coarse_rows, :]
    line = lax.broadcasted_iota(jnp.int32, (LANES * per, 1), 0)
    chunk = lax.div(lax.rem(line, per), 2)
    place = spread(rows_ref[...], per) + (chunk * coarse_rows).astype(F32)
    out_ref[...] = matmul(pick(place, chunks * coarse_rows), coarse[...]).astype(BF16)


def short_kernel(
    full_ref,
    before_ref,
    after_ref,
    short_ref,
    long_ref,
    send_ref,
    short_recv_ref,
    long_recv_ref,
    w_in_ref,
    b_in_ref,
    w_out_ref,
    b_out_ref,
    gain_ref,
    shift_ref,
    node_w_ref,
    node_b_ref,
    short_new_ref,
    long_pre_ref,
    sum_ref,
    node_pre_ref,
    own_ref,
    halo,
):
    chunks, rows, width = full_ref.shape
    quarter = own_ref.shape[0]
    latent = chunks * width
    start = pl.multiple_of(lax.axis_index("lat") * quarter, quarter)
    for c in range(chunks):
        lanes = slice(c * width, (c + 1) * width)
        halo[:HALO, lanes] = before_ref[c]
        halo[HALO : HALO + rows, lanes] = full_ref[c]
        halo[HALO + rows :, lanes] = after_ref[c]
        own_ref[:, lanes] = full_ref[c, pl.ds(start, quarter), :]
    own = own_ref[...]
    w_self = w_in_ref[:latent, :]
    w_send = w_in_ref[latent : 2 * latent, :]
    w_recv = w_in_ref[2 * latent :, :]
    recv_short = matmul(pick(columns(short_recv_ref[...]), quarter), own).astype(BF16)
    recv_long = matmul(pick(columns(long_recv_ref[...]), quarter), own).astype(BF16)
    sent = matmul(pick(columns(send_ref[...]), halo.shape[0]), halo[...]).astype(BF16)
    edges = short_ref[...]
    pre = matmul(edges, w_self) + matmul(sent, w_send) + matmul(recv_short, w_recv) + b_in_ref[...]
    hidden = silu(pre).astype(BF16)
    output = matmul(hidden, w_out_ref[...]) + b_out_ref[...]
    updated = (edges.astype(F32) + norm_rows(output, gain_ref[...], shift_ref[...])).astype(BF16)
    short_new_ref[...] = updated
    receivers = short_recv_ref[...]
    total = jnp.zeros((quarter, latent), F32)
    for i in range(receivers.shape[0]):
        mine = lax.broadcasted_iota(jnp.int32, (quarter, LANES), 0) == receivers[i : i + 1]
        hot = jnp.where(mine, 1.0, 0.0).astype(BF16)
        total = total + matmul(hot, updated[i * LANES : (i + 1) * LANES])
    sum_ref[...] = total
    long_pre_ref[...] = matmul(long_ref[...], w_self) + matmul(recv_long, w_recv) + b_in_ref[...]
    node_pre_ref[...] = matmul(own, node_w_ref[:latent, :]) + node_b_ref[...]


def long_kernel(
    far_ref,
    long_ref,
    long_pre_ref,
    sum_ref,
    node_pre_ref,
    own_ref,
    send_ref,
    recv_ref,
    w_in_ref,
    w_out_ref,
    b_out_ref,
    gain_ref,
    shift_ref,
    node_w_ref,
    node_w_out_ref,
    node_b_out_ref,
    node_gain_ref,
    node_shift_ref,
    long_new_ref,
    own_new_ref,
):
    chunks, quarter, width = own_new_ref.shape
    latent = chunks * width
    per = 2 * chunks
    send = columns(send_ref[...])
    source = jnp.floor(send * 0.5)
    place = source * per + (send - 2.0 * source)
    far = far_ref[...]
    pre = long_pre_ref[...]
    for c in range(chunks):
        sent = matmul(pick(place + 2.0 * c, far.shape[0]), far).astype(BF16)
        first = latent + c * width
        pre = pre + matmul(sent, w_in_ref[first : first + width, :])
    hidden = silu(pre).astype(BF16)
    output = matmul(hidden, w_out_ref[...]) + b_out_ref[...]
    updated = (long_ref[...].astype(F32) + norm_rows(output, gain_ref[...], shift_ref[...])).astype(BF16)
    long_new_ref[...] = updated
    mine = lax.broadcasted_iota(jnp.int32, (quarter, LANES), 0) == recv_ref[...]
    hot = jnp.where(mine, 1.0, 0.0).astype(BF16)
    aggregate = (sum_ref[...] + matmul(hot, updated)).astype(BF16)
    node_pre = node_pre_ref[...] + matmul(aggregate, node_w_ref[latent:, :])
    node_hidden = silu(node_pre).astype(BF16)
    node_out = matmul(node_hidden, node_w_out_ref[...]) + node_b_out_ref[...]
    new = own_ref[...].astype(F32) + norm_rows(node_out, node_gain_ref[...], node_shift_ref[...])
    new = new.astype(BF16)
    for c in range(chunks):
        own_new_ref[c] = new[:, c * width : (c + 1) * width]


def tile_kernel(rows_ref, index_ref, out_ref):
    out_ref[...] = matmul(pick(spread(index_ref[...], 2), rows_ref.shape[0]), rows_ref[...]).astype(BF16)


def call(kernel, outs, operands, flops, scratch=()):
    moved = sum(x.size * x.dtype.itemsize for x in (*operands, *outs))
    return pl.pallas_call(
        kernel,
        out_shape=tuple(outs),
        in_specs=[pl.BlockSpec(memory_space=pltpu.VMEM)] * len(operands),
        out_specs=tuple(pl.BlockSpec(memory_space=pltpu.VMEM) for _ in outs),
        scratch_shapes=list(scratch),
        compiler_params=pltpu.CompilerParams(vmem_limit_bytes=24 * 1024 * 1024),
        cost_estimate=pl.CostEstimate(flops=flops, bytes_accessed=moved, transcendentals=0),
    )(*operands)


def shape(dims, dtype=BF16):
    return jax.ShapeDtypeStruct(dims, dtype)


def body(
    nodes,
    short_edges,
    long_edges,
    short_send,
    short_recv,
    long_send,
    long_recv,
    send_rows,
    tile_rows,
    edge_w_in,
    edge_b_in,
    edge_w_out,
    edge_b_out,
    edge_gain,
    edge_shift,
    node_w_in,
    node_b_in,
    node_w_out,
    node_b_out,
    node_gain,
    node_shift,
):
    latent = edge_w_out.shape[0]
    rows, width = nodes.shape
    patches, lats = lax.axis_size("patch"), lax.axis_size("lat")
    quarter = rows // lats
    shorts, longs = short_edges.shape[0], long_edges.shape[0]
    row = lambda v: v.reshape(1, latent)

    copies = jnp.broadcast_to(nodes[None], (lats, rows, width))
    full = lax.all_to_all(copies, "lat", split_axis=0, concat_axis=0, tiled=True)

    (outgoing,) = call(
        functools.partial(far_kernel, coarse_rows=16),
        [shape((patches * 2 * lats, width))],
        [full, send_rows[0].T],
        2 * patches * 2 * lats * 64 * width,
        [pltpu.VMEM((lats * 16, width), BF16)],
    )
    outgoing = outgoing.reshape(patches, 2 * lats, width)
    arrived = lax.all_to_all(outgoing, "patch", split_axis=0, concat_axis=0, tiled=True)

    up = [(i, (i + 1) % patches) for i in range(patches)]
    down = [(j, i) for i, j in up]
    before = lax.ppermute(full[:, rows - HALO :], "patch", up)
    after = lax.ppermute(full[:, :HALO], "patch", down)
    short_new, long_pre, total, node_pre, own = call(
        short_kernel,
        [
            shape((shorts, latent)),
            shape((longs, latent), F32),
            shape((quarter, latent), F32),
            shape((quarter, latent), F32),
            shape((quarter, latent)),
        ],
        [
            full,
            before,
            after,
            short_edges,
            long_edges,
            short_send.reshape(-1, LANES),
            short_recv.reshape(-1, LANES),
            long_recv.reshape(-1, LANES),
            edge_w_in,
            row(edge_b_in),
            edge_w_out,
            row(edge_b_out),
            row(edge_gain),
            row(edge_shift),
            node_w_in,
            row(node_b_in),
        ],
        2 * 400 * 512 * 512 * 4,
        [pltpu.VMEM((rows + 2 * HALO, latent), BF16)],
    )
    long_new, own_new = call(
        long_kernel,
        [shape((longs, latent)), shape((lats, quarter, width))],
        [
            arrived.reshape(patches * 2 * lats, width),
            long_edges,
            long_pre,
            total,
            node_pre,
            own,
            long_send.reshape(-1, LANES),
            long_recv.reshape(-1, LANES),
            edge_w_in,
            edge_w_out,
            row(edge_b_out),
            row(edge_gain),
            row(edge_shift),
            node_w_in,
            node_w_out,
            row(node_b_out),
            row(node_gain),
            row(node_shift),
        ],
        2 * 200 * 512 * 512 * 4,
    )
    node_rows = lax.all_to_all(own_new, "lat", split_axis=0, concat_axis=0, tiled=True).reshape(rows, width)
    (tile_send,) = call(
        tile_kernel,
        [shape((patches * 2, width))],
        [node_rows, tile_rows[0].T],
        2 * patches * 2 * rows * width,
    )
    tiles = lax.all_to_all(
        tile_send.reshape(patches, 2, width), "patch", split_axis=0, concat_axis=0, tiled=True
    ).reshape(patches * 2, width)
    return (short_new, long_new, node_rows, tiles)


def solution(mesh):
    placed = (
        P("patch", "lat"),
        P(("patch", "lat"), None),
        P(("patch", "lat"), None),
        P(("patch", "lat")),
        P(("patch", "lat")),
        P(("patch", "lat")),
        P(("patch", "lat")),
        P("patch", None, None),
        P("patch", None, None),
    ) + (P(),) * 12
    return jax.shard_map(
        body,
        mesh=mesh,
        in_specs=placed,
        out_specs=(
            P(("patch", "lat"), None),
            P(("patch", "lat"), None),
            P("patch", "lat"),
            P("patch", "lat"),
        ),
        check_vma=False,
    )
```

```python
import functools

import jax
import jax.numpy as jnp
from jax import lax
from jax.experimental import pallas as pl
from jax.experimental.pallas import tpu as pltpu
from jax.sharding import PartitionSpec as P

HALO = 128
COARSE = 16
LIMITS = {"far": 56, "early": 52, "pack": 52, "main": 52, "tile": 8}
LANES = 128
F32 = jnp.float32
BF16 = jnp.bfloat16


def matmul(a, b):
    return jnp.dot(a, b, preferred_element_type=F32)


def silu(v):
    return v / (1.0 + jnp.exp(-v))


def norm_rows(values, gain_row, shift_row):
    average = jnp.mean(values, axis=-1, keepdims=True)
    centered = values - average
    variance = jnp.mean(centered * centered, axis=-1, keepdims=True)
    return centered * lax.rsqrt(variance + 1e-05) * gain_row + shift_row


def column(row):
    shape = (LANES, LANES)
    same = lax.broadcasted_iota(jnp.int32, shape, 0) == lax.broadcasted_iota(jnp.int32, shape, 1)
    return jnp.sum(jnp.where(same, row.astype(F32), 0.0), axis=1, keepdims=True)


def columns(rows):
    return jnp.concatenate([column(rows[i : i + 1]) for i in range(rows.shape[0])], axis=0)


def pick(index_column, count):
    shape = (index_column.shape[0], count)
    places = lax.broadcasted_iota(jnp.int32, shape, 1).astype(F32)
    return jnp.where(places == index_column, 1.0, 0.0).astype(BF16)


def spread(index_rows, repeat):
    shape = (LANES * repeat, LANES)
    line = lax.broadcasted_iota(jnp.int32, shape, 0)
    patch = lax.broadcasted_iota(jnp.int32, shape, 1)
    here = lax.div(line, repeat) == patch
    odd = lax.rem(line, 2) == 1
    values = jnp.where(odd, index_rows[1:2].astype(F32), index_rows[0:1].astype(F32))
    return jnp.sum(jnp.where(here, values, 0.0), axis=1, keepdims=True)


def fetch(pairs, sems, first=0):
    copies = [pltpu.make_async_copy(a, b, sems.at[first + i]) for i, (a, b) in enumerate(pairs)]
    for copy in copies:
        copy.start()
    return copies


def far_kernel(nodes_hbm, rows_hbm, far_ref, inner_ref, outer_ref, nodes, index, sems):
    copies = fetch([(rows_hbm, index), (nodes_hbm, nodes)], sems)
    copies[0].wait()
    hot = pick(spread(index[...], 2), COARSE)
    copies[1].wait()
    odd = lax.rem(lax.axis_index("patch"), 2)
    span = nodes.shape[0] - HALO
    inner_ref[...] = nodes[pl.ds(pl.multiple_of((1 - odd) * span, HALO), HALO), :]
    outer_ref[...] = nodes[pl.ds(pl.multiple_of(odd * span, HALO), HALO), :]
    far_ref[...] = matmul(hot, nodes[:COARSE, :]).astype(BF16)


def early_kernel(*refs, count, vectors):
    sources, (pre_ref, send_hot, far_hot, recv_hot, recv_cold, vec_ref) = (refs[:count], refs[count : count + 6])
    places, sems = (refs[count + 6 : -1], refs[-1])
    latent = pre_ref.shape[1]
    sources = list(sources)
    sources[0] = sources[0].at[:latent]
    order = list(range(3 + 1, count)) + [0, 3, 1, 2]
    copies = {i: pltpu.make_async_copy(sources[i], places[i], sems.at[i]) for i in order}
    for i in order:
        copies[i].start()
    w_self, short, long, b_in, short_send, short_recv, long_send, long_recv = places[:8]
    for i in range(4, count):
        copies[i].wait()
    for i in range(vectors):
        vec_ref[i : i + 1, :] = places[8 + i][...]
    shorts = short.shape[0]
    quarter = recv_hot.shape[1]
    send_hot[...] = pick(columns(short_send[...]), send_hot.shape[1])
    far_hot[...] = pick(columns(long_send[...]), far_hot.shape[1])
    recv_hot[:shorts, :] = pick(columns(short_recv[...]), quarter)
    recv_hot[shorts:, :] = pick(columns(long_recv[...]), quarter)
    receivers = [short_recv[i : i + 1, :] for i in range(short_recv.shape[0])]
    receivers += [long_recv[i : i + 1, :] for i in range(long_recv.shape[0])]
    for i, receiver in enumerate(receivers):
        mine = lax.broadcasted_iota(jnp.int32, (quarter, LANES), 0) == receiver
        recv_cold[:, i * LANES : (i + 1) * LANES] = jnp.where(mine, 1.0, 0.0).astype(BF16)
    for i in range(4):
        copies[i].wait()
    pre_ref[:shorts, :] = matmul(short[...], w_self[...]) + b_in[...]
    pre_ref[shorts:, :] = matmul(long[...], w_self[...]) + b_in[...]


def pack_kernel(nodes_hbm, inner_hbm, outer_hbm, far_hbm, out_hbm, sems):
    rows = nodes_hbm.shape[0]
    ends = HALO + rows
    odd = lax.rem(lax.axis_index("patch"), 2)
    inner = pl.multiple_of((1 - odd) * ends, HALO)
    outer = pl.multiple_of(odd * ends, HALO)
    pairs = []
    for c in range(out_hbm.shape[0]):
        pairs += [
            (far_hbm, out_hbm.at[c, pl.ds(ends + HALO, far_hbm.shape[0])]),
            (nodes_hbm, out_hbm.at[c, pl.ds(HALO, rows)]),
            (inner_hbm, out_hbm.at[c, pl.ds(inner, HALO)]),
            (outer_hbm, out_hbm.at[c, pl.ds(outer, HALO)]),
        ]
    for copy in fetch(pairs, sems):
        copy.wait()


def main_kernel(*refs, count):
    sources, (short_new_hbm, long_new_hbm, own_new_ref) = (refs[:count], refs[count : count + 3])
    places, (new_edges, sems) = (refs[count + 3 : -2], refs[-2:])
    full, send_hot, w_in, recv_hot, pre, far_hot, vec, w_out, short, long, recv_cold, node_w, node_w_out = places
    chunks, quarter, width = own_new_ref.shape
    latent = chunks * width
    copies = []
    for i in range(1, count):
        source = sources[i].at[latent:] if places[i] is w_in else sources[i]
        copies.append(pltpu.make_async_copy(source, places[i], sems.at[i]))
    first = [
        pltpu.make_async_copy(sources[0].at[c], full.at[:, pl.ds(c * width, width)], sems.at[count + c])
        for c in range(chunks)
    ]
    for copy in first + copies:
        copy.start()

    def ready(*wanted):
        for i, place in enumerate(places):
            if any(place is w for w in wanted):
                copies[i - 1].wait()

    shorts, near = send_hot.shape
    for copy in first:
        copy.wait()
    start = pl.multiple_of(lax.axis_index("lat") * quarter + HALO, quarter)
    own = full[pl.ds(start, quarter), :]
    ready(send_hot, far_hot, recv_hot)
    sents = (
        matmul(send_hot[...], full[:near, :]).astype(BF16),
        matmul(far_hot[...], full[near:, :]).astype(BF16),
    )
    received = matmul(recv_hot[...], own).astype(BF16)
    ready(w_in, pre, vec, w_out, short, long)
    b_out, gain, shift, node_b, node_b_out, node_gain, node_shift = (vec[i : i + 1, :] for i in range(7))
    parts = ((0, shorts, short, short_new_hbm), (shorts, pre.shape[0], long, long_new_hbm))
    stores = []
    for i, (low, high, edges, out_hbm) in enumerate(parts):
        before = pre[low:high, :] + matmul(sents[i], w_in[:latent, :]) + matmul(received[low:high], w_in[latent:, :])
        output = matmul(silu(before).astype(BF16), w_out[...]) + b_out
        new = edges[...].astype(F32) + norm_rows(output, gain, shift)
        new_edges[low:high, :] = new.astype(BF16)
        stores.append(pltpu.make_async_copy(new_edges.at[low:high], out_hbm, sems.at[count + chunks + i]))
        stores[-1].start()
    ready(recv_cold, node_w, node_w_out)
    aggregate = matmul(recv_cold[...], new_edges[...]).astype(BF16)
    node_pre = matmul(own, node_w[:latent, :]) + matmul(aggregate, node_w[latent:, :]) + node_b
    node_out = matmul(silu(node_pre).astype(BF16), node_w_out[...]) + node_b_out
    new = own.astype(F32) + norm_rows(node_out, node_gain, node_shift)
    new = new.astype(BF16)
    for c in range(chunks):
        own_new_ref[c] = new[:, c * width : (c + 1) * width]
    for copy in stores:
        copy.wait()


def tile_kernel(rows_ref, index_ref, out_ref):
    hot = pick(spread(index_ref[...], 2), rows_ref.shape[0])
    out_ref[...] = matmul(hot, rows_ref[...]).astype(BF16)


VMEM = pl.BlockSpec(memory_space=pltpu.VMEM)
ANY = pl.BlockSpec(memory_space=pl.ANY)
DMA = pltpu.SemaphoreType.DMA


def call(kernel, operands, outs, limit, flops, scratch=(), ins=ANY, out_specs=None):
    return pl.pallas_call(
        kernel,
        out_shape=tuple(outs),
        in_specs=[ins] * len(operands),
        out_specs=tuple(out_specs or [VMEM] * len(outs)),
        scratch_shapes=list(scratch),
        compiler_params=pltpu.CompilerParams(vmem_limit_bytes=limit * 1024 * 1024),
        cost_estimate=pl.CostEstimate(flops=flops, bytes_accessed=0, transcendentals=0),
    )(*operands)


def shape(dims, dtype=BF16):
    return jax.ShapeDtypeStruct(dims, dtype)


def like(arrays):
    return [pltpu.VMEM(x.shape, x.dtype) for x in arrays]


def body(
    nodes,
    short_edges,
    long_edges,
    short_send,
    short_recv,
    long_send,
    long_recv,
    send_rows,
    tile_rows,
    edge_w_in,
    edge_b_in,
    edge_w_out,
    edge_b_out,
    edge_gain,
    edge_shift,
    node_w_in,
    node_b_in,
    node_w_out,
    node_b_out,
    node_gain,
    node_shift,
):
    latent = edge_w_out.shape[0]
    rows, width = nodes.shape
    patches, lats = lax.axis_size("patch"), lax.axis_size("lat")
    slots = send_rows.shape[2]
    quarter = rows // lats
    shorts, longs = short_edges.shape[0], long_edges.shape[0]
    edges = shorts + longs
    near, far = rows + 2 * HALO, patches * slots

    outgoing, inner, outer = call(
        far_kernel,
        [nodes, send_rows[0].T],
        [shape((far, width)), shape((HALO, width)), shape((HALO, width))],
        LIMITS["far"],
        2 * far * COARSE * width,
        [pltpu.VMEM((rows, width), BF16), pltpu.VMEM((slots, patches), jnp.int32), DMA((2,))],
    )
    arrived = lax.all_to_all(
        outgoing.reshape(patches, slots, width), "patch", split_axis=0, concat_axis=0, tiled=True
    ).reshape(far, width)
    inner = lax.ppermute(inner, "patch", [(i, i ^ 1) for i in range(patches)])
    outer = lax.ppermute(outer, "patch", [(i, ((i + 1) ^ 1) - 1) for i in range(1, patches - 1)] + [(0, patches - 1), (patches - 1, 0)])
    (packed,) = call(
        pack_kernel,
        [nodes, inner, outer, arrived],
        [shape((lats, near + far, width))],
        LIMITS["pack"],
        0,
        [DMA((4 * lats,))],
        out_specs=[ANY],
    )
    full = lax.all_to_all(packed, "lat", split_axis=0, concat_axis=0, tiled=True)

    vectors = [v.reshape(1, latent) for v in (edge_b_out, edge_gain, edge_shift, node_b_in, node_b_out, node_gain, node_shift)]
    ints = [v.reshape(-1, LANES) for v in (short_send, short_recv, long_send, long_recv)]
    sources = [edge_w_in, short_edges, long_edges, edge_b_in.reshape(1, latent), *ints, *vectors]
    pre, send_hot, far_hot, recv_hot, recv_cold, vec = call(
        functools.partial(early_kernel, count=len(sources), vectors=len(vectors)),
        sources,
        [
            shape((edges, latent), F32),
            shape((shorts, near)),
            shape((longs, far)),
            shape((edges, quarter)),
            shape((quarter, edges)),
            shape((8, latent), F32),
        ],
        LIMITS["early"],
        2 * edges * latent * latent,
        [pltpu.VMEM((latent, latent), BF16)] + like(sources[1:]) + [DMA((len(sources),))],
    )
    sources = [full, send_hot, edge_w_in, recv_hot, pre, far_hot, vec, edge_w_out, short_edges, long_edges, recv_cold]
    sources += [node_w_in, node_w_out]
    places = [pltpu.VMEM((near + far, latent), BF16)] + like(sources[1:])
    places[2] = pltpu.VMEM((2 * latent, latent), BF16)
    short_new, long_new, own_new = call(
        functools.partial(main_kernel, count=len(sources)),
        sources,
        [shape((shorts, latent)), shape((longs, latent)), shape((lats, quarter, width))],
        LIMITS["main"],
        2 * edges * latent * latent * 5,
        places + [pltpu.VMEM((edges, latent), BF16), DMA((len(sources) + lats + 2,))],
        out_specs=[ANY, ANY, VMEM],
    )
    node_rows = lax.all_to_all(own_new, "lat", split_axis=0, concat_axis=0, tiled=True).reshape(rows, width)
    (tile_send,) = call(
        tile_kernel,
        [node_rows, tile_rows[0].T],
        [shape((far, width))],
        LIMITS["tile"],
        2 * far * rows * width,
        ins=VMEM,
    )
    tiles = lax.all_to_all(
        tile_send.reshape(patches, slots, width), "patch", split_axis=0, concat_axis=0, tiled=True
    ).reshape(far, width)

    return (short_new, long_new, node_rows, tiles)


def solution(mesh):
    placed = (
        P("patch", "lat"),
        P(("patch", "lat"), None),
        P(("patch", "lat"), None),
        P(("patch", "lat")),
        P(("patch", "lat")),
        P(("patch", "lat")),
        P(("patch", "lat")),
        P("patch", None, None),
        P("patch", None, None),
    ) + (P(),) * 12
    return jax.shard_map(
        body,
        mesh=mesh,
        in_specs=placed,
        out_specs=(
            P(("patch", "lat"), None),
            P(("patch", "lat"), None),
            P("patch", "lat"),
            P("patch", "lat"),
        ),
        check_vma=False,
    )
```

```python
import functools

import jax
import jax.numpy as jnp
from jax import lax
from jax.experimental import pallas as pl
from jax.experimental.pallas import tpu as pltpu
from jax.sharding import PartitionSpec as P

HALO = 128
COARSE = 16
LIMITS = {"far": 56, "early": 56, "pack": 52, "main": 52, "tile": 8}
LANES = 128
F32 = jnp.float32
BF16 = jnp.bfloat16


def matmul(a, b):
    return jnp.dot(a, b, preferred_element_type=F32)


def silu(v):
    return v / (1.0 + jnp.exp(-v))


def norm_rows(values, gain_row, shift_row):
    average = jnp.mean(values, axis=-1, keepdims=True)
    centered = values - average
    variance = jnp.mean(centered * centered, axis=-1, keepdims=True)
    return centered * lax.rsqrt(variance + 1e-05) * gain_row + shift_row


def column(row):
    shape = (LANES, LANES)
    same = lax.broadcasted_iota(jnp.int32, shape, 0) == lax.broadcasted_iota(jnp.int32, shape, 1)
    return jnp.sum(jnp.where(same, row.astype(F32), 0.0), axis=1, keepdims=True)


def columns(rows):
    return jnp.concatenate([column(rows[i : i + 1]) for i in range(rows.shape[0])], axis=0)


def pick(index_column, count):
    shape = (index_column.shape[0], count)
    places = lax.broadcasted_iota(jnp.int32, shape, 1).astype(F32)
    return jnp.where(places == index_column, 1.0, 0.0).astype(BF16)


def shift(power):
    return power.bit_length() - 1


def spread(index_rows, repeat):
    shape = (LANES * repeat, LANES)
    line = lax.broadcasted_iota(jnp.int32, shape, 0)
    patch = lax.broadcasted_iota(jnp.int32, shape, 1)
    here = (line >> shift(repeat)) == patch
    odd = (line & 1) == 1
    values = jnp.where(odd, index_rows[1:2].astype(F32), index_rows[0:1].astype(F32))
    return jnp.sum(jnp.where(here, values, 0.0), axis=1, keepdims=True)


def fetch(pairs, sems, first=0):
    copies = [pltpu.make_async_copy(a, b, sems.at[first + i]) for i, (a, b) in enumerate(pairs)]
    for copy in copies:
        copy.start()
    return copies


def far_kernel(nodes_hbm, rows_hbm, far_ref, inner_ref, outer_ref, nodes, index, sems):
    copies = fetch([(rows_hbm, index), (nodes_hbm, nodes)], sems)
    copies[0].wait()
    hot = pick(spread(index[...], 2), COARSE)
    copies[1].wait()
    odd = lax.rem(lax.axis_index("patch"), 2)
    span = nodes.shape[0] - HALO
    inner_ref[...] = nodes[pl.ds(pl.multiple_of((1 - odd) * span, HALO), HALO), :]
    outer_ref[...] = nodes[pl.ds(pl.multiple_of(odd * span, HALO), HALO), :]
    far_ref[...] = matmul(hot, nodes[:COARSE, :]).astype(BF16)


def early_kernel(*refs, count, vectors):
    sources, (pre_ref, send_hot, far_hot, recv_hot, recv_cold, vec_ref) = (refs[:count], refs[count : count + 6])
    places, sems = (refs[count + 6 : -1], refs[-1])
    latent = pre_ref.shape[1]
    sources = list(sources)
    sources[0] = sources[0].at[:latent]
    order = list(range(3 + 1, count)) + [0, 3, 1, 2]
    copies = {i: pltpu.make_async_copy(sources[i], places[i], sems.at[i]) for i in order}
    for i in order:
        copies[i].start()
    w_self, short, long, b_in, short_send, short_recv, long_send, long_recv = places[:8]
    for i in range(4, count):
        copies[i].wait()
    for i in range(vectors):
        vec_ref[i : i + 1, :] = places[8 + i][...]
    shorts = short.shape[0]
    quarter = recv_hot.shape[1]
    send_hot[...] = pick(columns(short_send[...]), send_hot.shape[1])
    far_hot[...] = pick(columns(long_send[...]), far_hot.shape[1])
    recv_hot[:shorts, :] = pick(columns(short_recv[...]), quarter)
    recv_hot[shorts:, :] = pick(columns(long_recv[...]), quarter)
    receivers = [short_recv[i : i + 1, :] for i in range(short_recv.shape[0])]
    receivers += [long_recv[i : i + 1, :] for i in range(long_recv.shape[0])]
    for i, receiver in enumerate(receivers):
        mine = lax.broadcasted_iota(jnp.int32, (quarter, LANES), 0) == receiver
        recv_cold[:, i * LANES : (i + 1) * LANES] = jnp.where(mine, 1.0, 0.0).astype(BF16)
    for i in range(4):
        copies[i].wait()
    pre_ref[:shorts, :] = matmul(short[...], w_self[...]) + b_in[...]
    pre_ref[shorts:, :] = matmul(long[...], w_self[...]) + b_in[...]


def pack_kernel(nodes_hbm, inner_hbm, outer_hbm, far_hbm, out_hbm, sems):
    rows = nodes_hbm.shape[0]
    ends = HALO + rows
    odd = lax.rem(lax.axis_index("patch"), 2)
    inner = pl.multiple_of((1 - odd) * ends, HALO)
    outer = pl.multiple_of(odd * ends, HALO)
    pairs = []
    for c in range(out_hbm.shape[0]):
        pairs += [
            (far_hbm, out_hbm.at[c, pl.ds(ends + HALO, far_hbm.shape[0])]),
            (nodes_hbm, out_hbm.at[c, pl.ds(HALO, rows)]),
            (inner_hbm, out_hbm.at[c, pl.ds(inner, HALO)]),
            (outer_hbm, out_hbm.at[c, pl.ds(outer, HALO)]),
        ]
    for copy in fetch(pairs, sems):
        copy.wait()


def main_kernel(*refs, count):
    sources, (short_new_hbm, long_new_hbm, tile_ref, *own_news) = (refs[:count], refs[count : count + 7])
    places, (new_edges, tile_hot, own_new, sems) = (refs[count + 7 : -4], refs[-4:])
    full, send_hot, w_in, recv_hot, pre, far_hot, vec, w_out, short, long, recv_cold, node_w, node_w_out, index = places
    chunks, quarter, width = own_new.shape
    latent = chunks * width
    copies = []
    for i in range(1, count):
        source = sources[i].at[latent:] if places[i] is w_in else sources[i]
        copies.append(pltpu.make_async_copy(source, places[i], sems.at[i]))
    first = [
        pltpu.make_async_copy(sources[0].at[c], full.at[:, pl.ds(c * width, width)], sems.at[count + c])
        for c in range(chunks)
    ]
    for copy in first + copies:
        copy.start()

    def ready(*wanted):
        for i, place in enumerate(places):
            if any(place is w for w in wanted):
                copies[i - 1].wait()

    shorts, near = send_hot.shape
    lat = lax.axis_index("lat")
    ready(index)
    tile_hot[...] = pick(spread(index[...], 2) - (lat * quarter).astype(F32), quarter)
    for copy in first:
        copy.wait()
    start = pl.multiple_of(lax.axis_index("lat") * quarter + HALO, quarter)
    own = full[pl.ds(start, quarter), :]
    ready(send_hot, far_hot, recv_hot)
    sents = (
        matmul(send_hot[...], full[:near, :]).astype(BF16),
        matmul(far_hot[...], full[near:, :]).astype(BF16),
    )
    received = matmul(recv_hot[...], own).astype(BF16)
    ready(w_in, pre, vec, w_out, short, long)
    b_out, gain, shift, node_b, node_b_out, node_gain, node_shift = (vec[i : i + 1, :] for i in range(7))
    parts = ((0, shorts, short, short_new_hbm), (shorts, pre.shape[0], long, long_new_hbm))
    stores = []
    for i, (low, high, edges, out_hbm) in enumerate(parts):
        before = pre[low:high, :] + matmul(sents[i], w_in[:latent, :]) + matmul(received[low:high], w_in[latent:, :])
        output = matmul(silu(before).astype(BF16), w_out[...]) + b_out
        new = edges[...].astype(F32) + norm_rows(output, gain, shift)
        new_edges[low:high, :] = new.astype(BF16)
        stores.append(pltpu.make_async_copy(new_edges.at[low:high], out_hbm, sems.at[count + chunks + i]))
        stores[-1].start()
    ready(recv_cold, node_w, node_w_out)
    aggregate = matmul(recv_cold[...], new_edges[...]).astype(BF16)
    node_pre = matmul(own, node_w[:latent, :]) + matmul(aggregate, node_w[latent:, :]) + node_b
    node_out = matmul(silu(node_pre).astype(BF16), node_w_out[...]) + node_b_out
    new = own.astype(F32) + norm_rows(node_out, node_gain, node_shift)
    new = new.astype(BF16)
    for c in range(chunks):
        own_new[c] = new[:, c * width : (c + 1) * width]
    for d in range(chunks):
        own_news[d][...] = own_new[lat ^ d]
    tile = matmul(tile_hot[...], new).astype(BF16)
    for c in range(chunks):
        tile_ref[c] = tile[:, c * width : (c + 1) * width]
    for copy in stores:
        copy.wait()


def tile_kernel(arrived_ref, out_ref):
    total = arrived_ref[0].astype(F32)
    for c in range(1, arrived_ref.shape[0]):
        total = total + arrived_ref[c].astype(F32)
    out_ref[...] = total.astype(BF16)


def rows_kernel(*refs):
    pieces, out_ref = (refs[:-1], refs[-1])
    count = len(pieces)
    lat = lax.axis_index("lat")
    for d in range(count):
        out_ref[lat ^ d] = pieces[d][...]


VMEM = pl.BlockSpec(memory_space=pltpu.VMEM)
ANY = pl.BlockSpec(memory_space=pl.ANY)
DMA = pltpu.SemaphoreType.DMA


def call(kernel, operands, outs, limit, flops, scratch=(), ins=ANY, out_specs=None):
    return pl.pallas_call(
        kernel,
        out_shape=tuple(outs),
        in_specs=[ins] * len(operands),
        out_specs=tuple(out_specs or [VMEM] * len(outs)),
        scratch_shapes=list(scratch),
        compiler_params=pltpu.CompilerParams(vmem_limit_bytes=limit * 1024 * 1024),
        cost_estimate=pl.CostEstimate(flops=flops, bytes_accessed=0, transcendentals=0),
    )(*operands)


def shape(dims, dtype=BF16):
    return jax.ShapeDtypeStruct(dims, dtype)


def like(arrays):
    return [pltpu.VMEM(x.shape, x.dtype) for x in arrays]


def body(
    nodes,
    short_edges,
    long_edges,
    short_send,
    short_recv,
    long_send,
    long_recv,
    send_rows,
    tile_rows,
    edge_w_in,
    edge_b_in,
    edge_w_out,
    edge_b_out,
    edge_gain,
    edge_shift,
    node_w_in,
    node_b_in,
    node_w_out,
    node_b_out,
    node_gain,
    node_shift,
):
    latent = edge_w_out.shape[0]
    rows, width = nodes.shape
    patches, lats = lax.axis_size("patch"), lax.axis_size("lat")
    slots = send_rows.shape[2]
    quarter = rows // lats
    shorts, longs = short_edges.shape[0], long_edges.shape[0]
    edges = shorts + longs
    near, far = rows + 2 * HALO, patches * slots

    outgoing, inner, outer = call(
        far_kernel,
        [nodes, send_rows[0].T],
        [shape((far, width)), shape((HALO, width)), shape((HALO, width))],
        LIMITS["far"],
        2 * far * COARSE * width,
        [pltpu.VMEM((rows, width), BF16), pltpu.VMEM((slots, patches), jnp.int32), DMA((2,))],
    )
    arrived = lax.all_to_all(
        outgoing.reshape(patches, slots, width), "patch", split_axis=0, concat_axis=0, tiled=True
    ).reshape(far, width)
    inner = lax.ppermute(inner, "patch", [(i, i ^ 1) for i in range(patches)])
    outer = lax.ppermute(outer, "patch", [(i, ((i + 1) ^ 1) - 1) for i in range(1, patches - 1)] + [(0, patches - 1), (patches - 1, 0)])
    vectors = [v.reshape(1, latent) for v in (edge_b_out, edge_gain, edge_shift, node_b_in, node_b_out, node_gain, node_shift)]
    ints = [v.reshape(-1, LANES) for v in (short_send, short_recv, long_send, long_recv)]
    sources = [edge_w_in, short_edges, long_edges, edge_b_in.reshape(1, latent), *ints, *vectors]
    pre, send_hot, far_hot, recv_hot, recv_cold, vec = call(
        functools.partial(early_kernel, count=len(sources), vectors=len(vectors)),
        sources,
        [
            shape((edges, latent), F32),
            shape((shorts, near)),
            shape((longs, far)),
            shape((edges, quarter)),
            shape((quarter, edges)),
            shape((8, latent), F32),
        ],
        LIMITS["early"],
        2 * edges * latent * latent,
        [pltpu.VMEM((latent, latent), BF16)] + like(sources[1:]) + [DMA((len(sources),))],
    )
    arrived, pre, send_hot, far_hot, recv_hot, recv_cold, vec = lax.optimization_barrier(
        (arrived, pre, send_hot, far_hot, recv_hot, recv_cold, vec)
    )
    (packed,) = call(
        pack_kernel,
        [nodes, inner, outer, arrived],
        [shape((lats, near + far, width))],
        LIMITS["pack"],
        0,
        [DMA((4 * lats,))],
        out_specs=[ANY],
    )
    full = lax.all_to_all(packed, "lat", split_axis=0, concat_axis=0, tiled=True)

    sources = [full, send_hot, edge_w_in, recv_hot, pre, far_hot, vec, edge_w_out, short_edges, long_edges, recv_cold]
    sources += [node_w_in, node_w_out, tile_rows[0].T]
    places = [pltpu.VMEM((near + far, latent), BF16)] + like(sources[1:])
    places[2] = pltpu.VMEM((2 * latent, latent), BF16)
    short_new, long_new, tile_send, *pieces = call(
        functools.partial(main_kernel, count=len(sources)),
        sources,
        [shape((shorts, latent)), shape((longs, latent)), shape((lats, far, width))] + [shape((quarter, width))] * lats,
        LIMITS["main"],
        2 * edges * latent * latent * 5,
        places
        + [
            pltpu.VMEM((edges, latent), BF16),
            pltpu.VMEM((far, quarter), BF16),
            pltpu.VMEM((lats, quarter, width), BF16),
            DMA((len(sources) + lats + 2,)),
        ],
        out_specs=[ANY, ANY] + [VMEM] * (1 + lats),
    )
    arrived = lax.all_to_all(
        tile_send.reshape(lats * patches, slots, width), ("lat", "patch"), split_axis=0, concat_axis=0, tiled=True
    ).reshape(lats, far, width)
    for d in range(1, lats):
        pieces[d] = lax.ppermute(pieces[d], "lat", [(i, i ^ d) for i in range(lats)])
    (node_rows,) = call(rows_kernel, pieces, [shape((lats, quarter, width))], 8, 10**9, ins=VMEM)
    node_rows = node_rows.reshape(rows, width)
    (tiles,) = call(tile_kernel, [arrived], [shape((far, width))], 8, 10**8, ins=VMEM)
    return (short_new, long_new, node_rows, tiles)


def solution(mesh):
    placed = (
        P("patch", "lat"),
        P(("patch", "lat"), None),
        P(("patch", "lat"), None),
        P(("patch", "lat")),
        P(("patch", "lat")),
        P(("patch", "lat")),
        P(("patch", "lat")),
        P("patch", None, None),
        P("patch", None, None),
    ) + (P(),) * 12
    return jax.shard_map(
        body,
        mesh=mesh,
        in_specs=placed,
        out_specs=(
            P(("patch", "lat"), None),
            P(("patch", "lat"), None),
            P("patch", "lat"),
            P("patch", "lat"),
        ),
        check_vma=False,
    )
```

```python
import functools

import jax
import jax.numpy as jnp
from jax import lax
from jax.experimental import pallas as pl
from jax.experimental.pallas import tpu as pltpu
from jax.sharding import PartitionSpec as P

HALO = 128
COARSE = 16
LIMITS = {"far": 56, "early": 56, "pack": 52, "main": 51, "tile": 8}
LANES = 128
F32 = jnp.float32
BF16 = jnp.bfloat16


def matmul(a, b):
    return jnp.dot(a, b, preferred_element_type=F32)


def silu(v):
    return v / (1.0 + jnp.exp(-v))


def norm_rows(values, gain_row, shift_row):
    average = jnp.mean(values, axis=-1, keepdims=True)
    centered = values - average
    variance = jnp.mean(centered * centered, axis=-1, keepdims=True)
    return centered * lax.rsqrt(variance + 1e-05) * gain_row + shift_row


def column(row):
    shape = (LANES, LANES)
    same = lax.broadcasted_iota(jnp.int32, shape, 0) == lax.broadcasted_iota(jnp.int32, shape, 1)
    return jnp.sum(jnp.where(same, row.astype(F32), 0.0), axis=1, keepdims=True)


def columns(rows):
    return jnp.concatenate([column(rows[i : i + 1]) for i in range(rows.shape[0])], axis=0)


def pick(index_column, count):
    shape = (index_column.shape[0], count)
    places = lax.broadcasted_iota(jnp.int32, shape, 1).astype(F32)
    return jnp.where(places == index_column, 1.0, 0.0).astype(BF16)


def shift(power):
    return power.bit_length() - 1


def spread(index_rows, repeat):
    shape = (LANES * repeat, LANES)
    line = lax.broadcasted_iota(jnp.int32, shape, 0)
    patch = lax.broadcasted_iota(jnp.int32, shape, 1)
    here = (line >> shift(repeat)) == patch
    odd = (line & 1) == 1
    values = jnp.where(odd, index_rows[1:2].astype(F32), index_rows[0:1].astype(F32))
    return jnp.sum(jnp.where(here, values, 0.0), axis=1, keepdims=True)


def fetch(pairs, sems, first=0):
    copies = [pltpu.make_async_copy(a, b, sems.at[first + i]) for i, (a, b) in enumerate(pairs)]
    for copy in copies:
        copy.start()
    return copies


def far_kernel(nodes_hbm, rows_hbm, far_ref, inner_ref, outer_ref, nodes, index, sems):
    copies = fetch([(rows_hbm, index), (nodes_hbm, nodes)], sems)
    copies[0].wait()
    hot = pick(spread(index[...], 2), COARSE)
    copies[1].wait()
    odd = lax.rem(lax.axis_index("patch"), 2)
    span = nodes.shape[0] - HALO
    inner_ref[...] = nodes[pl.ds(pl.multiple_of((1 - odd) * span, HALO), HALO), :]
    outer_ref[...] = nodes[pl.ds(pl.multiple_of(odd * span, HALO), HALO), :]
    far_ref[...] = matmul(hot, nodes[:COARSE, :]).astype(BF16)


def early_kernel(*refs, count, vectors):
    sources, (pre_ref, send_hot, far_hot, recv_hot, recv_cold, vec_ref) = (refs[:count], refs[count : count + 6])
    places, sems = (refs[count + 6 : -1], refs[-1])
    latent = pre_ref.shape[1]
    sources = list(sources)
    sources[0] = sources[0].at[:latent]
    order = list(range(3 + 1, count)) + [0, 3, 1, 2]
    copies = {i: pltpu.make_async_copy(sources[i], places[i], sems.at[i]) for i in order}
    for i in order:
        copies[i].start()
    w_self, short, long, b_in, short_send, short_recv, long_send, long_recv = places[:8]
    for i in range(4, count):
        copies[i].wait()
    for i in range(vectors):
        vec_ref[i : i + 1, :] = places[8 + i][...]
    shorts = short.shape[0]
    quarter = recv_hot.shape[1]
    send_hot[...] = pick(columns(short_send[...]), send_hot.shape[1])
    far_hot[...] = pick(columns(long_send[...]), far_hot.shape[1])
    recv_hot[:shorts, :] = pick(columns(short_recv[...]), quarter)
    recv_hot[shorts:, :] = pick(columns(long_recv[...]), quarter)
    receivers = [short_recv[i : i + 1, :] for i in range(short_recv.shape[0])]
    receivers += [long_recv[i : i + 1, :] for i in range(long_recv.shape[0])]
    for i, receiver in enumerate(receivers):
        mine = lax.broadcasted_iota(jnp.int32, (quarter, LANES), 0) == receiver
        recv_cold[:, i * LANES : (i + 1) * LANES] = jnp.where(mine, 1.0, 0.0).astype(BF16)
    for i in range(4):
        copies[i].wait()
    pre_ref[:shorts, :] = matmul(short[...], w_self[...]) + b_in[...]
    pre_ref[shorts:, :] = matmul(long[...], w_self[...]) + b_in[...]


def pack_kernel(nodes_hbm, inner_hbm, outer_hbm, far_hbm, out_hbm, sems):
    rows = nodes_hbm.shape[0]
    ends = HALO + rows
    odd = lax.rem(lax.axis_index("patch"), 2)
    inner = pl.multiple_of((1 - odd) * ends, HALO)
    outer = pl.multiple_of(odd * ends, HALO)
    pairs = []
    for c in range(out_hbm.shape[0]):
        pairs += [
            (far_hbm, out_hbm.at[c, pl.ds(ends + HALO, far_hbm.shape[0])]),
            (nodes_hbm, out_hbm.at[c, pl.ds(HALO, rows)]),
            (inner_hbm, out_hbm.at[c, pl.ds(inner, HALO)]),
            (outer_hbm, out_hbm.at[c, pl.ds(outer, HALO)]),
        ]
    for copy in fetch(pairs, sems):
        copy.wait()


def main_kernel(*refs, count):
    sources, (short_new_hbm, long_new_hbm, own_new_ref) = (refs[:count], refs[count : count + 3])
    places, (new_edges, sems) = (refs[count + 3 : -2], refs[-2:])
    full, send_hot, w_in, recv_hot, pre, far_hot, vec, w_out, short, long, recv_cold, node_w, node_w_out = places
    chunks, quarter, width = own_new_ref.shape
    latent = chunks * width
    copies = []
    for i in range(1, count):
        source = sources[i].at[latent:] if places[i] is w_in else sources[i]
        copies.append(pltpu.make_async_copy(source, places[i], sems.at[i]))
    first = [
        pltpu.make_async_copy(sources[0].at[c], full.at[:, pl.ds(c * width, width)], sems.at[count + c])
        for c in range(chunks)
    ]
    for copy in first + copies:
        copy.start()

    def ready(*wanted):
        for i, place in enumerate(places):
            if any(place is w for w in wanted):
                copies[i - 1].wait()

    shorts, near = send_hot.shape
    for copy in first:
        copy.wait()
    start = pl.multiple_of(lax.axis_index("lat") * quarter + HALO, quarter)
    own = full[pl.ds(start, quarter), :]
    ready(send_hot, far_hot, recv_hot)
    sents = (
        matmul(send_hot[...], full[:near, :]).astype(BF16),
        matmul(far_hot[...], full[near:, :]).astype(BF16),
    )
    received = matmul(recv_hot[...], own).astype(BF16)
    ready(w_in, pre, vec, w_out, short, long)
    b_out, gain, shift, node_b, node_b_out, node_gain, node_shift = (vec[i : i + 1, :] for i in range(7))
    parts = ((0, shorts, short, short_new_hbm), (shorts, pre.shape[0], long, long_new_hbm))
    stores = []
    for i, (low, high, edges, out_hbm) in enumerate(parts):
        before = pre[low:high, :] + matmul(sents[i], w_in[:latent, :]) + matmul(received[low:high], w_in[latent:, :])
        output = matmul(silu(before).astype(BF16), w_out[...]) + b_out
        new = edges[...].astype(F32) + norm_rows(output, gain, shift)
        new_edges[low:high, :] = new.astype(BF16)
        stores.append(pltpu.make_async_copy(new_edges.at[low:high], out_hbm, sems.at[count + chunks + i]))
        stores[-1].start()
    ready(recv_cold, node_w, node_w_out)
    aggregate = matmul(recv_cold[...], new_edges[...]).astype(BF16)
    node_pre = matmul(own, node_w[:latent, :]) + matmul(aggregate, node_w[latent:, :]) + node_b
    node_out = matmul(silu(node_pre).astype(BF16), node_w_out[...]) + node_b_out
    new = own.astype(F32) + norm_rows(node_out, node_gain, node_shift)
    new = new.astype(BF16)
    for c in range(chunks):
        own_new_ref[c] = new[:, c * width : (c + 1) * width]
    for copy in stores:
        copy.wait()


def tile_kernel(rows_ref, index_ref, out_ref):
    hot = pick(spread(index_ref[...], 2), rows_ref.shape[0])
    out_ref[...] = matmul(hot, rows_ref[...]).astype(BF16)


def out_kernel(rows_ref, arrived_ref, rows_out, tiles_out):
    rows_out[...] = rows_ref[...]
    tiles_out[...] = arrived_ref[...]


VMEM = pl.BlockSpec(memory_space=pltpu.VMEM)
ANY = pl.BlockSpec(memory_space=pl.ANY)
DMA = pltpu.SemaphoreType.DMA


def call(kernel, operands, outs, limit, flops, scratch=(), ins=ANY, out_specs=None):
    return pl.pallas_call(
        kernel,
        out_shape=tuple(outs),
        in_specs=[ins] * len(operands),
        out_specs=tuple(out_specs or [VMEM] * len(outs)),
        scratch_shapes=list(scratch),
        compiler_params=pltpu.CompilerParams(vmem_limit_bytes=limit * 1024 * 1024),
        cost_estimate=pl.CostEstimate(flops=flops, bytes_accessed=0, transcendentals=0),
    )(*operands)


def shape(dims, dtype=BF16):
    return jax.ShapeDtypeStruct(dims, dtype)


def like(arrays):
    return [pltpu.VMEM(x.shape, x.dtype) for x in arrays]


def body(
    nodes,
    short_edges,
    long_edges,
    short_send,
    short_recv,
    long_send,
    long_recv,
    send_rows,
    tile_rows,
    edge_w_in,
    edge_b_in,
    edge_w_out,
    edge_b_out,
    edge_gain,
    edge_shift,
    node_w_in,
    node_b_in,
    node_w_out,
    node_b_out,
    node_gain,
    node_shift,
):
    latent = edge_w_out.shape[0]
    rows, width = nodes.shape
    patches, lats = lax.axis_size("patch"), lax.axis_size("lat")
    slots = send_rows.shape[2]
    quarter = rows // lats
    shorts, longs = short_edges.shape[0], long_edges.shape[0]
    edges = shorts + longs
    near, far = rows + 2 * HALO, patches * slots

    outgoing, inner, outer = call(
        far_kernel,
        [nodes, send_rows[0].T],
        [shape((far, width)), shape((HALO, width)), shape((HALO, width))],
        LIMITS["far"],
        2 * far * COARSE * width,
        [pltpu.VMEM((rows, width), BF16), pltpu.VMEM((slots, patches), jnp.int32), DMA((2,))],
    )
    arrived = lax.all_to_all(
        outgoing.reshape(patches, slots, width), "patch", split_axis=0, concat_axis=0, tiled=True
    ).reshape(far, width)
    inner = lax.ppermute(inner, "patch", [(i, i ^ 1) for i in range(patches)])
    outer = lax.ppermute(outer, "patch", [(i, ((i + 1) ^ 1) - 1) for i in range(1, patches - 1)] + [(0, patches - 1), (patches - 1, 0)])
    vectors = [v.reshape(1, latent) for v in (edge_b_out, edge_gain, edge_shift, node_b_in, node_b_out, node_gain, node_shift)]
    ints = [v.reshape(-1, LANES) for v in (short_send, short_recv, long_send, long_recv)]
    sources = [edge_w_in, short_edges, long_edges, edge_b_in.reshape(1, latent), *ints, *vectors]
    pre, send_hot, far_hot, recv_hot, recv_cold, vec = call(
        functools.partial(early_kernel, count=len(sources), vectors=len(vectors)),
        sources,
        [
            shape((edges, latent), F32),
            shape((shorts, near)),
            shape((longs, far)),
            shape((edges, quarter)),
            shape((quarter, edges)),
            shape((8, latent), F32),
        ],
        LIMITS["early"],
        2 * edges * latent * latent,
        [pltpu.VMEM((latent, latent), BF16)] + like(sources[1:]) + [DMA((len(sources),))],
    )
    arrived, pre, send_hot, far_hot, recv_hot, recv_cold, vec = lax.optimization_barrier(
        (arrived, pre, send_hot, far_hot, recv_hot, recv_cold, vec)
    )
    (packed,) = call(
        pack_kernel,
        [nodes, inner, outer, arrived],
        [shape((lats, near + far, width))],
        LIMITS["pack"],
        0,
        [DMA((4 * lats,))],
        out_specs=[ANY],
    )
    full = lax.all_to_all(packed, "lat", split_axis=0, concat_axis=0, tiled=True)

    sources = [full, send_hot, edge_w_in, recv_hot, pre, far_hot, vec, edge_w_out, short_edges, long_edges, recv_cold]
    sources += [node_w_in, node_w_out]
    places = [pltpu.VMEM((near + far, latent), BF16)] + like(sources[1:])
    places[2] = pltpu.VMEM((2 * latent, latent), BF16)
    short_new, long_new, own_new = call(
        functools.partial(main_kernel, count=len(sources)),
        sources,
        [shape((shorts, latent)), shape((longs, latent)), shape((lats, quarter, width))],
        LIMITS["main"],
        2 * edges * latent * latent * 5,
        places + [pltpu.VMEM((edges, latent), BF16), DMA((len(sources) + lats + 2,))],
        out_specs=[ANY, ANY, VMEM],
    )
    node_rows = lax.all_to_all(own_new, "lat", split_axis=0, concat_axis=0, tiled=True).reshape(rows, width)
    (tile_send,) = call(
        tile_kernel,
        [node_rows, tile_rows[0].T],
        [shape((far, width))],
        LIMITS["tile"],
        2 * far * rows * width,
        ins=VMEM,
    )
    tiles = lax.all_to_all(
        tile_send.reshape(patches, slots, width), "patch", split_axis=0, concat_axis=0, tiled=True
    ).reshape(far, width)

    node_rows, tiles = call(
        out_kernel, [node_rows, tiles], [shape((rows, width)), shape((far, width))], 8, 2 * far * far * width, ins=VMEM
    )
    return (short_new, long_new, node_rows, tiles)


def solution(mesh):
    placed = (
        P("patch", "lat"),
        P(("patch", "lat"), None),
        P(("patch", "lat"), None),
        P(("patch", "lat")),
        P(("patch", "lat")),
        P(("patch", "lat")),
        P(("patch", "lat")),
        P("patch", None, None),
        P("patch", None, None),
    ) + (P(),) * 12
    return jax.shard_map(
        body,
        mesh=mesh,
        in_specs=placed,
        out_specs=(
            P(("patch", "lat"), None),
            P(("patch", "lat"), None),
            P("patch", "lat"),
            P("patch", "lat"),
        ),
        check_vma=False,
    )
```

```python
import functools

import jax
import jax.numpy as jnp
from jax import lax
from jax.experimental import pallas as pl
from jax.experimental.pallas import tpu as pltpu
from jax.sharding import PartitionSpec as P

HALO = 128
COARSE = 16
LIMITS = {"far": 56, "early": 56, "pack": 52, "main": 51, "tile": 8}
LANES = 128
F32 = jnp.float32
BF16 = jnp.bfloat16


def matmul(a, b):
    return jnp.dot(a, b, preferred_element_type=F32)


def silu(v):
    return v / (1.0 + jnp.exp(-v))


def norm_rows(values, gain_row, shift_row):
    average = jnp.mean(values, axis=-1, keepdims=True)
    centered = values - average
    variance = jnp.mean(centered * centered, axis=-1, keepdims=True)
    return centered * lax.rsqrt(variance + 1e-05) * gain_row + shift_row


def column(row):
    shape = (LANES, LANES)
    same = lax.broadcasted_iota(jnp.int32, shape, 0) == lax.broadcasted_iota(jnp.int32, shape, 1)
    return jnp.sum(jnp.where(same, row.astype(F32), 0.0), axis=1, keepdims=True)


def columns(rows):
    return jnp.concatenate([column(rows[i : i + 1]) for i in range(rows.shape[0])], axis=0)


def pick(index_column, count):
    shape = (index_column.shape[0], count)
    places = lax.broadcasted_iota(jnp.int32, shape, 1).astype(F32)
    return jnp.where(places == index_column, 1.0, 0.0).astype(BF16)


def shift(power):
    return power.bit_length() - 1


def spread(index_rows, repeat):
    shape = (LANES * repeat, LANES)
    line = lax.broadcasted_iota(jnp.int32, shape, 0)
    patch = lax.broadcasted_iota(jnp.int32, shape, 1)
    here = (line >> shift(repeat)) == patch
    odd = (line & 1) == 1
    values = jnp.where(odd, index_rows[1:2].astype(F32), index_rows[0:1].astype(F32))
    return jnp.sum(jnp.where(here, values, 0.0), axis=1, keepdims=True)


def fetch(pairs, sems, first=0):
    copies = [pltpu.make_async_copy(a, b, sems.at[first + i]) for i, (a, b) in enumerate(pairs)]
    for copy in copies:
        copy.start()
    return copies


def far_kernel(nodes_hbm, rows_hbm, far_ref, inner_ref, outer_ref, nodes, index, sems):
    copies = fetch([(rows_hbm, index), (nodes_hbm, nodes)], sems)
    copies[0].wait()
    hot = pick(spread(index[...], 2), COARSE)
    copies[1].wait()
    odd = lax.rem(lax.axis_index("patch"), 2)
    span = nodes.shape[0] - HALO
    inner_ref[...] = nodes[pl.ds(pl.multiple_of((1 - odd) * span, HALO), HALO), :]
    outer_ref[...] = nodes[pl.ds(pl.multiple_of(odd * span, HALO), HALO), :]
    far_ref[...] = matmul(hot, nodes[:COARSE, :]).astype(BF16)


def early_kernel(*refs, count, vectors):
    sources, (pre_ref, send_hot, far_hot, recv_hot, recv_cold, vec_ref) = (refs[:count], refs[count : count + 6])
    places, sems = (refs[count + 6 : -1], refs[-1])
    latent = pre_ref.shape[1]
    sources = list(sources)
    sources[0] = sources[0].at[:latent]
    order = list(range(3 + 1, count)) + [0, 3, 1, 2]
    copies = {i: pltpu.make_async_copy(sources[i], places[i], sems.at[i]) for i in order}
    for i in order:
        copies[i].start()
    w_self, short, long, b_in, short_send, short_recv, long_send, long_recv = places[:8]
    for i in range(4, count):
        copies[i].wait()
    for i in range(vectors):
        vec_ref[i : i + 1, :] = places[8 + i][...]
    shorts = short.shape[0]
    quarter = recv_hot.shape[1]
    send_hot[...] = pick(columns(short_send[...]), send_hot.shape[1])
    far_hot[...] = pick(columns(long_send[...]), far_hot.shape[1])
    recv_hot[:shorts, :] = pick(columns(short_recv[...]), quarter)
    recv_hot[shorts:, :] = pick(columns(long_recv[...]), quarter)
    receivers = [short_recv[i : i + 1, :] for i in range(short_recv.shape[0])]
    receivers += [long_recv[i : i + 1, :] for i in range(long_recv.shape[0])]
    for i, receiver in enumerate(receivers):
        mine = lax.broadcasted_iota(jnp.int32, (quarter, LANES), 0) == receiver
        recv_cold[:, i * LANES : (i + 1) * LANES] = jnp.where(mine, 1.0, 0.0).astype(BF16)
    for i in range(4):
        copies[i].wait()
    pre_ref[:shorts, :] = matmul(short[...], w_self[...]) + b_in[...]
    pre_ref[shorts:, :] = matmul(long[...], w_self[...]) + b_in[...]


def pack_kernel(nodes_hbm, inner_hbm, outer_hbm, far_hbm, out_hbm, sems):
    rows = nodes_hbm.shape[0]
    ends = HALO + rows
    odd = lax.rem(lax.axis_index("patch"), 2)
    inner = pl.multiple_of((1 - odd) * ends, HALO)
    outer = pl.multiple_of(odd * ends, HALO)
    pairs = []
    for c in range(out_hbm.shape[0]):
        pairs += [
            (far_hbm, out_hbm.at[c, pl.ds(ends + HALO, far_hbm.shape[0])]),
            (nodes_hbm, out_hbm.at[c, pl.ds(HALO, rows)]),
            (inner_hbm, out_hbm.at[c, pl.ds(inner, HALO)]),
            (outer_hbm, out_hbm.at[c, pl.ds(outer, HALO)]),
        ]
    for copy in fetch(pairs, sems):
        copy.wait()


def main_kernel(*refs, count):
    sources, (short_new_hbm, long_new_hbm, own_new_ref) = (refs[:count], refs[count : count + 3])
    places, (new_edges, sems) = (refs[count + 3 : -2], refs[-2:])
    full, send_hot, w_in, recv_hot, pre, far_hot, vec, w_out, short, long, recv_cold, node_w, node_w_out = places
    chunks, quarter, width = own_new_ref.shape
    latent = chunks * width
    copies = []
    for i in range(1, count):
        source = sources[i].at[latent:] if places[i] is w_in else sources[i]
        copies.append(pltpu.make_async_copy(source, places[i], sems.at[i]))
    first = [
        pltpu.make_async_copy(sources[0].at[c], full.at[:, pl.ds(c * width, width)], sems.at[count + c])
        for c in range(chunks)
    ]
    for copy in first + copies:
        copy.start()

    def ready(*wanted):
        for i, place in enumerate(places):
            if any(place is w for w in wanted):
                copies[i - 1].wait()

    shorts, near = send_hot.shape
    for copy in first:
        copy.wait()
    start = pl.multiple_of(lax.axis_index("lat") * quarter + HALO, quarter)
    own = full[pl.ds(start, quarter), :]
    ready(send_hot, far_hot, recv_hot)
    sents = (
        matmul(send_hot[...], full[:near, :]).astype(BF16),
        matmul(far_hot[...], full[near:, :]).astype(BF16),
    )
    received = matmul(recv_hot[...], own).astype(BF16)
    ready(w_in, pre, vec, w_out, short, long, recv_cold, node_w, node_w_out)
    b_out, gain, shift, node_b, node_b_out, node_gain, node_shift = (vec[i : i + 1, :] for i in range(7))
    sent = jnp.concatenate(sents, axis=0)
    edges = jnp.concatenate([short[...], long[...]], axis=0)
    own_pre = matmul(own, node_w[:latent, :]) + node_b
    before = pre[...] + matmul(sent, w_in[:latent, :]) + matmul(received, w_in[latent:, :])
    output = matmul(silu(before).astype(BF16), w_out[...]) + b_out
    new_edges[...] = (edges.astype(F32) + norm_rows(output, gain, shift)).astype(BF16)
    stores = []
    for i, (low, high, out_hbm) in enumerate(((0, shorts, short_new_hbm), (shorts, pre.shape[0], long_new_hbm))):
        stores.append(pltpu.make_async_copy(new_edges.at[low:high], out_hbm, sems.at[count + chunks + i]))
        stores[-1].start()
    aggregate = matmul(recv_cold[...], new_edges[...]).astype(BF16)
    node_pre = own_pre + matmul(aggregate, node_w[latent:, :])
    node_out = matmul(silu(node_pre).astype(BF16), node_w_out[...]) + node_b_out
    new = own.astype(F32) + norm_rows(node_out, node_gain, node_shift)
    new = new.astype(BF16)
    for c in range(chunks):
        own_new_ref[c] = new[:, c * width : (c + 1) * width]
    for copy in stores:
        copy.wait()


def tile_kernel(rows_ref, index_ref, out_ref):
    hot = pick(spread(index_ref[...], 2), rows_ref.shape[0])
    out_ref[...] = matmul(hot, rows_ref[...]).astype(BF16)


def out_kernel(rows_ref, arrived_ref, rows_out, tiles_out):
    rows_out[...] = rows_ref[...]
    tiles_out[...] = arrived_ref[...]


VMEM = pl.BlockSpec(memory_space=pltpu.VMEM)
ANY = pl.BlockSpec(memory_space=pl.ANY)
DMA = pltpu.SemaphoreType.DMA


def call(kernel, operands, outs, limit, flops, scratch=(), ins=ANY, out_specs=None):
    return pl.pallas_call(
        kernel,
        out_shape=tuple(outs),
        in_specs=[ins] * len(operands),
        out_specs=tuple(out_specs or [VMEM] * len(outs)),
        scratch_shapes=list(scratch),
        compiler_params=pltpu.CompilerParams(vmem_limit_bytes=limit * 1024 * 1024),
        cost_estimate=pl.CostEstimate(flops=flops, bytes_accessed=0, transcendentals=0),
    )(*operands)


def shape(dims, dtype=BF16):
    return jax.ShapeDtypeStruct(dims, dtype)


def like(arrays):
    return [pltpu.VMEM(x.shape, x.dtype) for x in arrays]


def body(
    nodes,
    short_edges,
    long_edges,
    short_send,
    short_recv,
    long_send,
    long_recv,
    send_rows,
    tile_rows,
    edge_w_in,
    edge_b_in,
    edge_w_out,
    edge_b_out,
    edge_gain,
    edge_shift,
    node_w_in,
    node_b_in,
    node_w_out,
    node_b_out,
    node_gain,
    node_shift,
):
    latent = edge_w_out.shape[0]
    rows, width = nodes.shape
    patches, lats = lax.axis_size("patch"), lax.axis_size("lat")
    slots = send_rows.shape[2]
    quarter = rows // lats
    shorts, longs = short_edges.shape[0], long_edges.shape[0]
    edges = shorts + longs
    near, far = rows + 2 * HALO, patches * slots

    outgoing, inner, outer = call(
        far_kernel,
        [nodes, send_rows[0].T],
        [shape((far, width)), shape((HALO, width)), shape((HALO, width))],
        LIMITS["far"],
        2 * far * COARSE * width,
        [pltpu.VMEM((rows, width), BF16), pltpu.VMEM((slots, patches), jnp.int32), DMA((2,))],
    )
    arrived = lax.all_to_all(
        outgoing.reshape(patches, slots, width), "patch", split_axis=0, concat_axis=0, tiled=True
    ).reshape(far, width)
    inner = lax.ppermute(inner, "patch", [(i, i ^ 1) for i in range(patches)])
    outer = lax.ppermute(outer, "patch", [(i, ((i + 1) ^ 1) - 1) for i in range(1, patches - 1)] + [(0, patches - 1), (patches - 1, 0)])
    vectors = [v.reshape(1, latent) for v in (edge_b_out, edge_gain, edge_shift, node_b_in, node_b_out, node_gain, node_shift)]
    ints = [v.reshape(-1, LANES) for v in (short_send, short_recv, long_send, long_recv)]
    sources = [edge_w_in, short_edges, long_edges, edge_b_in.reshape(1, latent), *ints, *vectors]
    pre, send_hot, far_hot, recv_hot, recv_cold, vec = call(
        functools.partial(early_kernel, count=len(sources), vectors=len(vectors)),
        sources,
        [
            shape((edges, latent), F32),
            shape((shorts, near)),
            shape((longs, far)),
            shape((edges, quarter)),
            shape((quarter, edges)),
            shape((8, latent), F32),
        ],
        LIMITS["early"],
        2 * edges * latent * latent,
        [pltpu.VMEM((latent, latent), BF16)] + like(sources[1:]) + [DMA((len(sources),))],
    )
    arrived, pre, send_hot, far_hot, recv_hot, recv_cold, vec = lax.optimization_barrier(
        (arrived, pre, send_hot, far_hot, recv_hot, recv_cold, vec)
    )
    (packed,) = call(
        pack_kernel,
        [nodes, inner, outer, arrived],
        [shape((lats, near + far, width))],
        LIMITS["pack"],
        0,
        [DMA((4 * lats,))],
        out_specs=[ANY],
    )
    full = lax.all_to_all(packed, "lat", split_axis=0, concat_axis=0, tiled=True)

    sources = [full, send_hot, edge_w_in, recv_hot, pre, far_hot, vec, edge_w_out, short_edges, long_edges, recv_cold]
    sources += [node_w_in, node_w_out]
    places = [pltpu.VMEM((near + far, latent), BF16)] + like(sources[1:])
    places[2] = pltpu.VMEM((2 * latent, latent), BF16)
    short_new, long_new, own_new = call(
        functools.partial(main_kernel, count=len(sources)),
        sources,
        [shape((shorts, latent)), shape((longs, latent)), shape((lats, quarter, width))],
        LIMITS["main"],
        2 * edges * latent * latent * 5,
        places + [pltpu.VMEM((edges, latent), BF16), DMA((len(sources) + lats + 2,))],
        out_specs=[ANY, ANY, VMEM],
    )
    node_rows = lax.all_to_all(own_new, "lat", split_axis=0, concat_axis=0, tiled=True).reshape(rows, width)
    (tile_send,) = call(
        tile_kernel,
        [node_rows, tile_rows[0].T],
        [shape((far, width))],
        LIMITS["tile"],
        2 * far * rows * width,
        ins=VMEM,
    )
    tiles = lax.all_to_all(
        tile_send.reshape(patches, slots, width), "patch", split_axis=0, concat_axis=0, tiled=True
    ).reshape(far, width)

    node_rows, tiles = call(
        out_kernel, [node_rows, tiles], [shape((rows, width)), shape((far, width))], 8, 2 * far * far * width, ins=VMEM
    )
    return (short_new, long_new, node_rows, tiles)


def solution(mesh):
    placed = (
        P("patch", "lat"),
        P(("patch", "lat"), None),
        P(("patch", "lat"), None),
        P(("patch", "lat")),
        P(("patch", "lat")),
        P(("patch", "lat")),
        P(("patch", "lat")),
        P("patch", None, None),
        P("patch", None, None),
    ) + (P(),) * 12
    return jax.shard_map(
        body,
        mesh=mesh,
        in_specs=placed,
        out_specs=(
            P(("patch", "lat"), None),
            P(("patch", "lat"), None),
            P("patch", "lat"),
            P("patch", "lat"),
        ),
        check_vma=False,
    )
```
